256 devices in a mesh: group: 16 (over x_lo, y, core), loop: 16 (over x_hi, z).
Axes of the slice: x: 4 (x_hi: 2, x_lo: 2; x = x_hi * 2 + x_lo), y: 4, z: 8, core: 2. Of those that a mesh axis runs over, the one named last changes fastest.
Arguments:
- images: bfloat16 [32768, 1152], P(('group', 'loop')), may hold values from -1.5 to 1.5
- texts: bfloat16 [32768, 1152], P(('group', 'loop')), may hold values from -1.5 to 1.5
- logit_scale: float32 [1], replicated, may hold values from 80 to 120
- logit_bias: float32 [1], replicated, may hold values from -15 to -12
Outputs:
- loss: float32 [], replicated
- grad_images: float32 [32768, 1152], P(('group', 'loop'))
- grad_texts: float32 [32768, 1152], P(('group', 'loop'))
The draws below stay inside these ranges and needn't reach their ends.
All inputs are finite; a program needn't handle non-finite values.
Results may differ from the reference program's by a relative error of at most 0.003.
The reference program's roundings to bfloat16 on the way (of `pair_grad`) count: a program that leaves them out, or rounds other values in their place, can miss the bound.
Values may be sent and summed in bfloat16 or wider, within the bound.
A program may use at most 64 MiB of HBM per device.

```python
import math
import jax
import jax.numpy as jnp
from jax import lax

D = 1152
ROWS_DEV = 128
BATCH = 32768
STEPS = 8
WINDOW = 16384
N_GROUP = 16
N_LOOP = 16


def pair_fields(key):
    keys = jax.random.split(key, 5)
    image_normal = jnp.clip(jax.random.normal(keys[0], (BATCH, D), jnp.float32), -4.0, 4.0)
    text_normal = jnp.clip(jax.random.normal(keys[2], (BATCH, D), jnp.float32), -4.0, 4.0)
    image_noise = image_normal
    text_noise = text_normal
    position = jnp.arange(BATCH, dtype=jnp.float32)[:, None] / BATCH
    ranking = 0.5 * position + 0.5 * jax.random.uniform(keys[4], (BATCH, 1), jnp.float32)
    coupling = 0.05 + 0.55 * ranking
    image_dir = image_noise
    text_dir = coupling * image_noise + jnp.sqrt(1.0 - coupling * coupling) * text_noise
    return (image_dir, text_dir)


def draw_images(key, part):
    low_scale = 0.5
    image_dir, text_dir = pair_fields(key)
    own_key = jax.random.fold_in(key, 11)
    row_scale = jnp.exp(jax.random.uniform(own_key, (BATCH, 1), jnp.float32, math.log(low_scale), math.log(4.0)))
    return (0.05 * row_scale * image_dir).astype(jnp.bfloat16)


def draw_texts(key, part):
    low_scale = 0.5
    image_dir, text_dir = pair_fields(key)
    own_key = jax.random.fold_in(key, 23)
    row_scale = jnp.exp(jax.random.uniform(own_key, (BATCH, 1), jnp.float32, math.log(low_scale), math.log(4.0)))
    return (0.05 * row_scale * text_dir).astype(jnp.bfloat16)


def setup_inputs(seed: int = 0) -> dict:
    splits = jax.random.split(jax.random.key(seed), 5)
    images = draw_images(jax.random.fold_in(splits[4], 71), 0)
    texts = draw_texts(jax.random.fold_in(splits[4], 71), 0)
    logit_scale = jnp.clip(jnp.exp(jax.random.uniform(splits[2], (1,), jnp.float32, math.log(80.0), math.log(120.0))), 80.0, 120.0)
    logit_bias = jnp.clip(jax.random.uniform(splits[3], (1,), jnp.float32, -15.0, -12.0), -15.0, -12.0)
    return {"images": images, "texts": texts, "logit_scale": logit_scale, "logit_bias": logit_bias}


def unit_rows(raw):
    wide = raw.astype(jnp.float32)
    norm = jnp.sqrt(lax.optimization_barrier(jnp.sum(wide * wide, axis=1, keepdims=True)) + 1e-06)
    return (wide / norm, norm)

def back_norm(unit, norm, grad):
    return (grad - unit * lax.optimization_barrier(jnp.sum(unit * grad, axis=1, keepdims=True))) / norm

def reference(images, texts, logit_scale, logit_bias):
    scale = logit_scale[0]
    bias = logit_bias[0]
    image_unit, image_norm = unit_rows(images)
    text_unit, text_norm = unit_rows(texts)
    image_low = image_unit.astype(jnp.bfloat16)
    text_low = text_unit.astype(jnp.bfloat16)
    blocks = BATCH // ROWS_DEV
    image_blocks = image_low.reshape(blocks, ROWS_DEV, D)
    text_four = text_low.reshape(N_GROUP, N_LOOP, ROWS_DEV, D)
    doubled = jnp.concatenate([text_four, text_four], axis=1)
    columns = jnp.arange(WINDOW, dtype=jnp.int32)
    col_group = columns // (STEPS * ROWS_DEV)
    col_step = columns // ROWS_DEV % STEPS
    col_row = columns % ROWS_DEV
    row_ids = jnp.arange(ROWS_DEV, dtype=jnp.int32)
    anchor = jnp.zeros((), jnp.int32)

    def one_block(carry, inputs):
        text_acc, loss_acc = carry
        block, index = inputs
        group_here = (index // N_LOOP).astype(jnp.int32)
        loop_here = (index % N_LOOP).astype(jnp.int32)
        starts = (anchor, loop_here, anchor, anchor)
        window = lax.dynamic_slice(doubled, starts, (N_GROUP, STEPS, ROWS_DEV, D)).reshape(WINDOW, D)
        logits = scale * jnp.dot(block, window.T, preferred_element_type=jnp.float32) + bias
        positive = (col_group[None, :] == group_here) & (col_step[None, :] == 0) & (col_row[None, :] == row_ids[:, None])
        sign = jnp.where(positive, 1.0, -1.0).astype(jnp.float32)
        loss_acc = loss_acc + jnp.sum(jax.nn.softplus(-sign * logits))
        pair_grad = (-sign * jax.nn.sigmoid(-sign * logits) * scale).astype(jnp.bfloat16)
        image_part = jnp.dot(pair_grad, window, preferred_element_type=jnp.float32)
        text_part = jnp.dot(pair_grad.T, block, preferred_element_type=jnp.float32).reshape(N_GROUP, STEPS, ROWS_DEV, D)
        current = lax.dynamic_slice(text_acc, starts, (N_GROUP, STEPS, ROWS_DEV, D))
        text_acc = lax.dynamic_update_slice(text_acc, current + text_part, starts)
        return ((text_acc, loss_acc), image_part)
    start_carry = (jnp.zeros((N_GROUP, 2 * N_LOOP, ROWS_DEV, D), jnp.float32), jnp.zeros((), jnp.float32))
    (text_acc, total), image_parts = lax.scan(one_block, start_carry, (image_blocks, jnp.arange(blocks, dtype=jnp.int32)))
    text_grad = (text_acc[:, :N_LOOP] + text_acc[:, N_LOOP:]).reshape(BATCH, D)
    image_grad = image_parts.reshape(BATCH, D)
    loss = total / BATCH
    return (loss, back_norm(image_unit, image_norm, image_grad), back_norm(text_unit, text_norm, text_grad))
```

```python
import jax
import jax.numpy as jnp
from jax import lax
from jax.experimental import pallas as pl
from jax.experimental.pallas import tpu as pltpu
from jax.sharding import PartitionSpec as P

MESH = pl.DeviceIdType.MESH
F32 = jnp.float32
LOW = jnp.bfloat16
ROWS = 128
HALF = 64
WIDTH = 1152
CHUNK = 4 * ROWS
NT = (((1,), (1,)), ((), ()))
NN = (((1,), (0,)), ((), ()))
TN = (((0,), (0,)), ((), ()))
A, B = 0, 1
(NEXT, PREV, BACK, UNBACK, YUP, YDOWN, YFAR, CORE, LO, MIRROR, XFAR, ZPAIR, ZUP2, ZDOWN2, ZFAR) = range(15)
GREETED = (NEXT, PREV, BACK, UNBACK, YUP, YDOWN, YFAR, CORE, LO, MIRROR, XFAR, ZUP2, ZDOWN2, ZFAR)
(
    F1, F2, F3, F4, B1, B2, B3, B4, S0, S1, S2, S3, S4, S5, S6, S7, G0, G1, G2, G3, G4, G5, G6, G7,
    TU, TD, TX, TXU, TXD, T2U, T2D, T3X, CF0, CF1, CF2, CF3, CB0, CB1, CB2, CB3,
    X1, X2, Y1U, Y1D, Y0U, Y0D, Y3U, Y3D,
    LC, LX, LM, LF, LYU, LYD, LYF, LZ, LZU, LZD, LZF, LAST,
) = range(0, 120, 2)
HALVED = (
    F1, F2, F3, B1, B2, B3, S0, S1, S2, S3, S4, S5, S6, S7, TU, TD, TX, TXU, TXD, T3X,
    CF0, CF1, CF2, CB0, CB1, CB2, X1, X2, Y1U, Y1D, Y0U, Y0D,
)
SENT = (
    [hop + h for hop in HALVED for h in (A, B)]
    + [F4 + A, B4 + B, T2U + A, T2D + B, CF3 + A, CB3 + B, Y3U + A, Y3D + B]
    + list(range(G0, G7 + 1, 2))
    + list(range(LC, LZF + 1, 2))
)
VISITS = {
    F1: (0, 1, NEXT), F2: (1, 3, NEXT), F3: (3, 5, NEXT), F4: (5, 7, NEXT),
    B1: (0, 2, BACK), B2: (2, 4, PREV), B3: (4, 6, PREV), B4: (6, 7, PREV),
}
OWN, SIDE, UP, DOWN, FAR, SIDE_UP, SIDE_DOWN, SIDE_FAR = range(8)
TEXTS = {
    TU: (OWN, DOWN, YUP), TD: (OWN, UP, YDOWN), TX: (OWN, SIDE, LO),
    T2U: (DOWN, FAR, YUP), T2D: (UP, FAR, YDOWN),
    TXU: (SIDE, SIDE_DOWN, YUP), TXD: (SIDE, SIDE_UP, YDOWN), T3X: (FAR, SIDE_FAR, LO),
}
SUMS = {
    CF0: (0, PREV), CF1: (1, PREV), CF2: (2, PREV), CF3: (3, PREV),
    CB0: (4, UNBACK), CB1: (5, NEXT), CB2: (6, NEXT), CB3: (7, NEXT),
    X1: (8, LO), X2: (9, LO), Y1U: (10, YUP), Y1D: (11, YDOWN),
    Y0U: (12, YUP), Y0D: (13, YDOWN), Y3U: (14, YUP), Y3D: (14, YDOWN),
}
LOSSES = {
    LC: (0, 0, CORE), LX: (1, 1, LO), LM: (1, 2, MIRROR), LF: (1, 3, XFAR),
    LYU: (2, 4, YUP), LYD: (2, 5, YDOWN), LYF: (2, 6, YFAR),
    LZ: (3, 7, ZPAIR), LZU: (4, 8, ZUP2), LZD: (4, 9, ZDOWN2), LZF: (4, 10, ZFAR),
}


def dot(a, b, dims):
    return lax.dot_general(a, b, dims, preferred_element_type=F32)


def unit_rows(raw):
    wide = raw.astype(F32)
    norm = jnp.sqrt(jnp.sum(wide * wide, axis=1, keepdims=True) + 1e-06)
    return wide / norm, norm


def back_norm(unit, norm, grad):
    return (grad - unit * jnp.sum(unit * grad, axis=1, keepdims=True)) / norm


def devices():
    g, l = lax.axis_index("group"), lax.axis_index("loop")
    core, y, lo = g % 2, (g // 2) % 4, g // 8
    z, hi = l % 8, l // 8

    def at(lo=lo, y=y, core=core, hi=hi, z=z):
        return ((lo * 4 + y) * 2 + core, hi * 8 + z)

    def flip(bit, when):
        return jnp.where(when, 1 - bit, bit)

    up, down = (z + 1) % 8, (z + 7) % 8
    return {
        NEXT: at(lo=flip(lo, z == 7), hi=flip(hi, z == 7), z=up),
        PREV: at(lo=flip(lo, z == 0), hi=flip(hi, z == 0), z=down),
        BACK: at(lo=flip(lo, z != 0), hi=flip(hi, z != 0), z=down),
        UNBACK: at(lo=flip(lo, z != 7), hi=flip(hi, z != 7), z=up),
        YUP: at(y=(y + 1) % 4),
        YDOWN: at(y=(y + 3) % 4),
        YFAR: at(y=(y + 2) % 4),
        CORE: at(core=1 - core),
        LO: at(lo=1 - lo),
        MIRROR: at(lo=1 - lo, hi=1 - hi),
        XFAR: at(hi=1 - hi),
        ZPAIR: at(z=z + 1 - 2 * (z % 2)),
        ZUP2: at(z=(z + 2) % 8),
        ZDOWN2: at(z=(z + 6) % 8),
        ZFAR: at(z=(z + 4) % 8),
    }


def kernel(
    scale_ref, bias_ref, img_ref, txt_ref, loss_ref, gimg_ref, gtxt_ref,
    raw, unit, V, T, gI, sI, rI, gT, out, arrived, lacc, lout, lin, lsem, ssem, rsem,
):
    dev = devices()
    scale, bias = scale_ref[0], bias_ref[0]
    loads = [pltpu.make_async_copy(ref, raw.at[i], lsem.at[i]) for i, ref in enumerate((img_ref, txt_ref))]
    for load in loads:
        load.start()

    barrier = pltpu.get_barrier_semaphore()
    for to in GREETED:
        pl.semaphore_signal(barrier, inc=1, device_id=dev[to], device_id_type=MESH)

    def rows(i, h):
        return pl.ds(i * ROWS + h * HALF, HALF)

    def copy(name):
        h, base = name % 2, name - name % 2
        if base in VISITS:
            s, d, to = VISITS[base]
            src, dst = V.at[s, rows(0, h)], V.at[d, rows(0, h)]
        elif base in TEXTS:
            s, d, to = TEXTS[base]
            src, dst = T.at[rows(s, h)], T.at[rows(d, h)]
        elif base in SUMS:
            k, to = SUMS[base]
            src, dst = out.at[k, rows(0, h)], arrived.at[k, rows(0, h)]
        elif base in LOSSES:
            s, d, to = LOSSES[base]
            src, dst = lout.at[s], lin.at[d]
        elif base >= G0:
            s, to = (base - G0) // 2, CORE
            src, dst = sI.at[s], rI.at[s]
        else:
            s, to = (base - S0) // 2, CORE
            src, dst = V.at[s, rows(0, h)], V.at[s, rows(1, h)]
        return pltpu.make_async_remote_copy(
            src_ref=src, dst_ref=dst, send_sem=ssem.at[name], recv_sem=rsem.at[name],
            device_id=dev[to], device_id_type=MESH,
        )

    def start(*names):
        for name in names:
            copy(name).start()

    def got(*names):
        for name in names:
            copy(name).wait_recv()

    def passes(name, *onward):
        got(name)
        start(*onward)

    def pair_terms(logits, positive):
        y = jnp.where(positive, -logits, logits)
        e = jnp.exp(-jnp.abs(y))
        u = 1.0 + e
        r = 1.0 / u
        grad = jnp.where(y >= 0, r, e * r) * scale
        grad = jnp.where(positive, -grad, grad)
        log_term = jnp.where(e < 0.01, e * (1.0 - e * (0.5 - e * (1.0 / 3.0))), jnp.log(u))
        return grad.astype(LOW), jnp.maximum(y, 0.0) + log_term

    def tile(s, c, own):
        texts = pl.ds(pl.multiple_of(c * CHUNK, CHUNK), CHUNK)
        v, t = V[s], T[texts]
        logits = scale * dot(v, t, NT) + bias
        row = lax.broadcasted_iota(jnp.int32, logits.shape, 0)
        col = lax.broadcasted_iota(jnp.int32, logits.shape, 1)
        g, loss = pair_terms(logits, (row == col) & (row < jnp.where(own, ROWS, 0)))
        lacc[...] += jnp.sum(loss.reshape(-1, 8, CHUNK), axis=0)
        gT[texts] += dot(g, v, TN)
        part = dot(g, t, NN)
        gI[s] += part[:ROWS]
        sI[s] += part[ROWS:]

    def send_image(name, s, *more):
        k, h = SUMS[name - name % 2][0], name % 2
        total = gI[s, rows(0, h)] + rI[s, rows(0, h)]
        for m in more:
            got(m + h)
            total += arrived[SUMS[m][0], rows(0, h)].astype(F32)
        out[k, rows(0, h)] = total.astype(LOW)
        start(name)

    def send_text(name, block, *more):
        k, h = SUMS[name - name % 2][0], name % 2
        total = gT[rows(block, h)]
        for m in more:
            got(m + h)
            total += arrived[SUMS[m][0], rows(0, h)].astype(F32)
        out[k, rows(0, h)] = total.astype(LOW)
        start(name)

    for i in range(2):
        loads[i].wait()
        unit[i] = unit_rows(raw[i])[0]
    V[0, :ROWS] = unit[0].astype(LOW)
    T[:ROWS] = unit[1].astype(LOW)
    pl.semaphore_wait(barrier, len(GREETED))
    start(F1 + A, B1 + B, TU + A, TD + B, TX + A, S0 + A)
    start(F1 + B, B1 + A, TU + B, TD + A, TX + B, S0 + B)
    gT[...] = jnp.zeros_like(gT)
    gI[...] = jnp.zeros_like(gI)
    sI[...] = jnp.zeros_like(sI)
    lacc[...] = jnp.zeros_like(lacc)

    passes(F1 + A, F2 + A, S1 + A)
    passes(B1 + B, B2 + B, S2 + B)
    passes(TU + A, T2U + A)
    passes(TD + B, T2D + B)
    passes(TX + A, TXU + A, TXD + A)
    passes(F1 + B, F2 + B, S1 + B)
    passes(B1 + A, B2 + A, S2 + A)
    passes(TX + B, TXU + B, TXD + B)
    got(TU + B, TD + A, S0 + A, S0 + B)

    def serve_0():
        got(S1 + A, S1 + B)

    def serve_1():
        passes(F2 + A, F3 + A, S3 + A)
        passes(B2 + B, B3 + B, S4 + B)
        passes(T2U + A, T3X + A)
        passes(T2D + B, T3X + B)
        got(S2 + A, S2 + B)

    def serve_2():
        passes(F2 + B, F3 + B, S3 + B)
        passes(B2 + A, B3 + A, S4 + A)
        got(S3 + A, S3 + B)

    def serve_3():
        passes(F3 + A, F4 + A, S5 + A)
        passes(B3 + B, B4 + B, S6 + B)
        got(S4 + A, S4 + B)

    def serve_4():
        got(TXU + A, TXD + A, TXU + B, TXD + B, T3X + A, T3X + B)

    def serve_5():
        start(G3)
        passes(F3 + B, S5 + B)
        passes(B3 + A, S6 + A)

    def serve_6():
        start(G4)
        got(S5 + A, S5 + B)
        passes(F4 + A, S7 + A)
        passes(B4 + B, S7 + B)

    def serve_8():
        start(G5)
        got(S7 + A, S7 + B)

    def serve_9():
        got(G5)
        send_image(CF2 + B, 5)

    def serve_10():
        start(G7)
        got(S6 + A, S6 + B)

    def serve_11():
        got(G7)
        send_image(CF3 + A, 7)
        send_image(CB3 + B, 7)

    def serve_12():
        start(G6)
        send_text(Y0U + B, UP)
        send_text(Y0D + A, DOWN)

    def serve_13():
        start(G1)
        got(G6)
        send_image(CB2 + A, 6)
        got(G3)
        send_image(CF1 + B, 3, CF2)

    def serve_14():
        start(G2)
        send_image(CF2 + A, 5, CF3)
        send_image(CB2 + B, 6, CB3)

    def serve_15():
        start(G0)

    served = {
        0: serve_0, 1: serve_1, 2: serve_2, 3: serve_3, 4: serve_4, 5: serve_5, 6: serve_6, 8: serve_8,
        9: serve_9, 10: serve_10, 11: serve_11, 12: serve_12, 13: serve_13, 14: serve_14, 15: serve_15,
    }
    order = ((0, 0), (1, 0), (2, 0), (3, 0), (4, 0), (3, 1), (4, 1), (5, 1),
             (5, 0), (7, 1), (7, 0), (6, 1), (6, 0), (1, 1), (2, 1), (0, 1))

    def picked(i, values):
        number = values[-1]
        for k in range(len(values) - 2, -1, -1):
            number = jnp.where(i == k, values[k], number)
        return number

    def step(i, carry):
        tile(picked(i, [s for s, c in order]), picked(i, [c for s, c in order]), i == 0)
        for k, serve in served.items():
            pl.when(i == k)(serve)
        return carry

    lax.fori_loop(0, len(order), step, 0)

    for h in (A, B):
        send_text(X1 + h, SIDE_FAR)
        send_text(Y1U + h, SIDE_UP)
        send_text(Y1D + h, SIDE_DOWN)
    lout[0] = sum(lacc[:, c : c + 128] for c in range(0, CHUNK, 128))
    start(LC)
    got(G4)
    send_image(CB1 + A, 4, CB2)
    got(G1)
    send_image(CF0 + B, 1, CF1)
    got(LC)
    lout[1] = lout[0] + lin[0]
    start(LX, LM, LF)
    send_image(CF1 + A, 3, CF2)
    send_image(CB1 + B, 4, CB2)
    send_text(Y3U + A, FAR, X1)
    send_text(Y3D + B, FAR, X1)
    got(LX, LM, LF)
    lout[2] = (lout[1] + lin[1]) + (lin[2] + lin[3])
    start(LYU, LYD, LYF)
    got(G2)
    send_image(CB0 + A, 2, CB1)
    send_text(X2 + A, SIDE, Y1U, Y1D)
    send_text(X2 + B, SIDE, Y1U, Y1D)
    got(LYU, LYD, LYF)
    lout[3] = (lout[2] + lin[6]) + (lin[4] + lin[5])
    start(LZ)
    send_image(CF0 + A, 1, CF1)
    send_image(CB0 + B, 2, CB1)
    send_text(Y0U + A, UP, Y3U)
    send_text(Y0D + B, DOWN, Y3D)
    got(LZ)
    lout[4] = lout[3] + lin[7]
    start(LZU, LZD, LZF)

    def finish(i, total, ref, *more):
        for m in more:
            got(m + A, m + B)
            total += arrived[SUMS[m][0]].astype(F32)
        ref[...] = back_norm(unit[i], unit_rows(raw[i])[1], total)

    got(G0)
    finish(0, gI[0] + rI[0], gimg_ref, CF0, CB0)
    finish(1, gT[:ROWS], gtxt_ref, X2, Y0U, Y0D)
    got(LZU, LZD, LZF)
    total = (lout[4] + lin[10]) + (lin[8] + lin[9])
    batch = ROWS * lax.axis_size("group") * lax.axis_size("loop")
    loss_ref[...] = jnp.sum(total, keepdims=True).reshape(1, 1) / batch
    for name in SENT:
        copy(name).wait_send()


def body(images, texts, logit_scale, logit_bias):
    vmem = pl.BlockSpec(memory_space=pltpu.VMEM)
    smem = pl.BlockSpec(memory_space=pltpu.SMEM)
    hbm = pl.BlockSpec(memory_space=pl.ANY)
    block = (ROWS, WIDTH)
    loss, grad_images, grad_texts = pl.pallas_call(
        kernel,
        out_shape=(
            jax.ShapeDtypeStruct((1, 1), F32),
            jax.ShapeDtypeStruct(block, F32),
            jax.ShapeDtypeStruct(block, F32),
        ),
        in_specs=[smem, smem, hbm, hbm],
        out_specs=(vmem, vmem, vmem),
        scratch_shapes=[
            pltpu.VMEM((2,) + block, LOW),
            pltpu.VMEM((2,) + block, F32),
            pltpu.VMEM((8, 2 * ROWS, WIDTH), LOW),
            pltpu.VMEM((8 * ROWS, WIDTH), LOW),
            pltpu.VMEM((8,) + block, F32),
            pltpu.VMEM((8,) + block, F32),
            pltpu.VMEM((8,) + block, F32),
            pltpu.VMEM((8 * ROWS, WIDTH), F32),
            pltpu.VMEM((15,) + block, LOW),
            pltpu.VMEM((15,) + block, LOW),
            pltpu.VMEM((8, CHUNK), F32),
            pltpu.VMEM((5, 8, 128), F32),
            pltpu.VMEM((11, 8, 128), F32),
            pltpu.SemaphoreType.DMA((2,)),
            pltpu.SemaphoreType.DMA((LAST,)),
            pltpu.SemaphoreType.DMA((LAST,)),
        ],
        compiler_params=pltpu.CompilerParams(
            collective_id=0, has_side_effects=True, vmem_limit_bytes=60 * 2**20
        ),
    )(logit_scale, logit_bias, images, texts)
    return loss.reshape(()), grad_images, grad_texts


def solution(mesh):
    rows = P(("group", "loop"), None)
    return jax.shard_map(
        body,
        mesh=mesh,
        in_specs=(rows, rows, P(), P()),
        out_specs=(P(), rows, rows),
        check_vma=False,
    )
```

```python
import jax
import jax.numpy as jnp
from jax import lax
from jax.experimental import pallas as pl
from jax.experimental.pallas import tpu as pltpu
from jax.sharding import PartitionSpec as P

MESH = pl.DeviceIdType.MESH
F32 = jnp.float32
LOW = jnp.bfloat16
ROWS = 128
HALF = 64
WIDTH = 1152
CHUNK = 4 * ROWS
NT = (((1,), (1,)), ((), ()))
NN = (((1,), (0,)), ((), ()))
TN = (((0,), (0,)), ((), ()))
A, B = 0, 1
(
    NEXT, PREV, BACK, UNBACK, YUP, YDOWN, YFAR, CORE, LO, MIRROR, XFAR, ZPAIR, Z2, Z4, Z6, DEVICES,
) = range(16)
(
    F1, F2, F3, F4, B1, B2, B3, B4, S0, S1, S2, S3, S4, S5, S6, S7, G0, G1, G2, G3, G4, G5, G6, G7,
    TU, TD, TX, TXU, TXD, T2, T3X, CF0, CF1, CF2, CF3, CB0, CB1, CB2, CB3,
    X1, X2, Y1U, Y1D, Y0U, Y0D, Y3U, Y3D,
    LOSS,
) = range(0, 96, 2)
LAST = LOSS + 11
HALVED = (
    F1, F2, F3, B1, B2, B3, S0, S1, S2, S3, S4, S5, S6, S7, TU, TD, TX, TXU, TXD, T2, T3X,
    CF0, CF1, CF2, CB0, CB1, CB2, X1, X2, Y1U, Y1D, Y0U, Y0D,
)
SENT = (
    [hop + h for hop in HALVED for h in (A, B)]
    + [F4 + A, B4 + B, CF3 + A, CB3 + B, Y3U + A, Y3D + B]
    + list(range(G0, G7 + 1, 2))
    + list(range(LOSS, LAST))
)
VISITS = {
    F1: (0, 1, NEXT), F2: (1, 3, NEXT), F3: (3, 5, NEXT), F4: (5, 7, NEXT),
    B1: (0, 2, BACK), B2: (2, 4, PREV), B3: (4, 6, PREV), B4: (6, 7, PREV),
}
OWN, SIDE, UP, DOWN, FAR, SIDE_UP, SIDE_DOWN, SIDE_FAR = range(8)
TEXTS = {
    TU: (OWN, DOWN, YUP), TD: (OWN, UP, YDOWN), TX: (OWN, SIDE, LO),
    T2: (OWN, FAR, YFAR),
    TXU: (SIDE, SIDE_DOWN, YUP), TXD: (SIDE, SIDE_UP, YDOWN), T3X: (FAR, SIDE_FAR, LO),
}
SUMS = {
    CF0: (0, PREV), CF1: (1, PREV), CF2: (2, PREV), CF3: (3, PREV),
    CB0: (4, UNBACK), CB1: (5, NEXT), CB2: (6, NEXT), CB3: (7, NEXT),
    X1: (8, LO), X2: (9, LO), Y1U: (10, YUP), Y1D: (11, YDOWN),
    Y0U: (12, YUP), Y0D: (13, YDOWN), Y3U: (14, YUP), Y3D: (14, YDOWN),
}
ROUNDS = (
    (CORE,),
    (LO, XFAR, MIRROR),
    (YFAR, YUP, YDOWN),
    (ZPAIR,),
    (Z4, Z2, Z6),
)
LOSSES = [(r, to) for r, partners in enumerate(ROUNDS) for to in partners]


def dot(a, b, dims):
    return lax.dot_general(a, b, dims, preferred_element_type=F32)


def unit_rows(raw):
    wide = raw.astype(F32)
    norm = jnp.sqrt(jnp.sum(wide * wide, axis=1, keepdims=True) + 1e-06)
    return wide / norm, norm


def back_norm(unit, norm, grad):
    return (grad - unit * jnp.sum(unit * grad, axis=1, keepdims=True)) / norm


def devices():
    g, l = lax.axis_index("group"), lax.axis_index("loop")
    core, y, lo = g % 2, (g // 2) % 4, g // 8
    z, hi = l % 8, l // 8

    def at(lo=lo, y=y, core=core, hi=hi, z=z):
        return ((lo * 4 + y) * 2 + core, hi * 8 + z)

    def flip(bit, when):
        return jnp.where(when, 1 - bit, bit)

    up, down = (z + 1) % 8, (z + 7) % 8
    return {
        NEXT: at(lo=flip(lo, z == 7), hi=flip(hi, z == 7), z=up),
        PREV: at(lo=flip(lo, z == 0), hi=flip(hi, z == 0), z=down),
        BACK: at(lo=flip(lo, z != 0), hi=flip(hi, z != 0), z=down),
        UNBACK: at(lo=flip(lo, z != 7), hi=flip(hi, z != 7), z=up),
        YUP: at(y=(y + 1) % 4),
        YDOWN: at(y=(y + 3) % 4),
        YFAR: at(y=(y + 2) % 4),
        CORE: at(core=1 - core),
        LO: at(lo=1 - lo),
        MIRROR: at(lo=1 - lo, hi=1 - hi),
        XFAR: at(hi=1 - hi),
        ZPAIR: at(z=z + 1 - 2 * (z % 2)),
        Z2: at(z=(z + 2) % 8),
        Z4: at(z=(z + 4) % 8),
        Z6: at(z=(z + 6) % 8),
    }


def kernel(
    scale_ref, bias_ref, img_ref, txt_ref, loss_ref, gimg_ref, gtxt_ref,
    raw, unit, V, T, gI, sI, rI, gT, out, arrived, lacc, lout, lin, lsem, ssem, rsem,
):
    dev = devices()
    scale, bias = scale_ref[0], bias_ref[0]
    loads = [pltpu.make_async_copy(ref, raw.at[i], lsem.at[i]) for i, ref in enumerate((img_ref, txt_ref))]
    for load in loads:
        load.start()

    barrier = pltpu.get_barrier_semaphore()
    for to in range(DEVICES):
        pl.semaphore_signal(barrier, inc=1, device_id=dev[to], device_id_type=MESH)

    def rows(i, h):
        return pl.ds(i * ROWS + h * HALF, HALF)

    def copy(name):
        h, base = name % 2, name - name % 2
        if name >= LOSS:
            r, to = LOSSES[name - LOSS]
            src, dst = lout.at[r], lin.at[name - LOSS]
        elif base in VISITS:
            s, d, to = VISITS[base]
            src, dst = V.at[s, rows(0, h)], V.at[d, rows(0, h)]
        elif base in TEXTS:
            s, d, to = TEXTS[base]
            src, dst = T.at[rows(s, h)], T.at[rows(d, h)]
        elif base in SUMS:
            k, to = SUMS[base]
            src, dst = out.at[k, rows(0, h)], arrived.at[k, rows(0, h)]
        elif base >= G0:
            s, to = (base - G0) // 2, CORE
            src, dst = sI.at[s], rI.at[s]
        else:
            s, to = (base - S0) // 2, CORE
            src, dst = V.at[s, rows(0, h)], V.at[s, rows(1, h)]
        return pltpu.make_async_remote_copy(
            src_ref=src, dst_ref=dst, send_sem=ssem.at[name], recv_sem=rsem.at[name],
            device_id=dev[to], device_id_type=MESH,
        )

    def start(*names):
        for name in names:
            copy(name).start()

    def got(*names):
        for name in names:
            copy(name).wait_recv()

    def passes(name, *onward):
        got(name)
        start(*onward)

    def pair_terms(logits):
        w = jnp.exp(jnp.minimum(logits, 80.0))
        u = 1.0 + w
        prob = w * (1.0 / u)
        log_term = jnp.where(w < 0.01, w * (1.0 - w * (0.5 - w * (1.0 / 3.0))), jnp.log(u))
        return prob, jnp.maximum(logits, log_term)

    def tile(s, texts, own=False):
        v, t = V[s], T[texts]
        logits = scale * dot(v, t, NT) + bias
        if own:
            row = lax.broadcasted_iota(jnp.int32, logits.shape, 0)
            col = lax.broadcasted_iota(jnp.int32, logits.shape, 1)
            positive = (row == col) & (row < ROWS)
            prob, loss = pair_terms(jnp.where(positive, -logits, logits))
            prob = jnp.where(positive, -prob, prob)
        else:
            prob, loss = pair_terms(logits)
        g = (prob * scale).astype(LOW)
        lacc[:, : t.shape[0]] += jnp.sum(loss.reshape(-1, 8, t.shape[0]), axis=0)
        gT[texts] += dot(g, v, TN)
        return dot(g, t, NN)

    def half_tile(s, c, own=False):
        part = tile(s, pl.ds(pl.multiple_of(c * CHUNK, CHUNK), CHUNK), own)
        gI[s] += part[:ROWS]
        sI[s] += part[ROWS:]

    def whole_tile(s):
        part = tile(s, pl.ds(0, 2 * CHUNK))
        gI[s] = part[:ROWS]
        sI[s] = part[ROWS:]

    def send_image(name, s, *more):
        k, h = SUMS[name - name % 2][0], name % 2
        total = gI[s, rows(0, h)] + rI[s, rows(0, h)]
        for m in more:
            got(m + h)
            total += arrived[SUMS[m][0], rows(0, h)].astype(F32)
        out[k, rows(0, h)] = total.astype(LOW)
        start(name)

    def send_text(name, block, *more):
        k, h = SUMS[name - name % 2][0], name % 2
        total = gT[rows(block, h)]
        for m in more:
            got(m + h)
            total += arrived[SUMS[m][0], rows(0, h)].astype(F32)
        out[k, rows(0, h)] = total.astype(LOW)
        start(name)

    for i in range(2):
        loads[i].wait()
        unit[i] = unit_rows(raw[i])[0]
    V[0, :ROWS] = unit[0].astype(LOW)
    T[:ROWS] = unit[1].astype(LOW)
    pl.semaphore_wait(barrier, DEVICES)
    start(F1 + A, B1 + B, TU + A, TD + B, TX + A, S0 + A)
    start(F1 + B, B1 + A, TU + B, TD + A, TX + B, S0 + B)
    start(T2 + A, T2 + B)
    gT[...] = jnp.zeros_like(gT)
    gI[:5] = jnp.zeros_like(gI[:5])
    sI[:5] = jnp.zeros_like(sI[:5])
    lacc[...] = jnp.zeros_like(lacc)

    passes(F1 + A, F2 + A, S1 + A)
    passes(B1 + B, B2 + B, S2 + B)
    got(TU + A, TD + B, TU + B, TD + A, S0 + A, S0 + B)
    passes(TX + A, TXU + A, TXD + A)
    passes(TX + B, TXU + B, TXD + B)
    half_tile(0, 0, True)
    passes(F1 + B, F2 + B, S1 + B)
    passes(B1 + A, B2 + A, S2 + A)
    got(S1 + A, S1 + B)

    def after_1():
        passes(T2 + A, T3X + A)
        passes(T2 + B, T3X + B)
        passes(F2 + A, F3 + A, S3 + A)
        passes(B2 + B, B3 + B, S4 + B)
        got(S2 + A, S2 + B)

    def after_2():
        passes(F2 + B, F3 + B, S3 + B)
        passes(B2 + A, B3 + A, S4 + A)
        got(S3 + A, S3 + B)

    def after_3():
        passes(F3 + A, F4 + A, S5 + A)
        passes(B3 + B, B4 + B, S6 + B)
        got(S4 + A, S4 + B)

    def after_4():
        got(TXU + A, TXD + A, TXU + B, TXD + B, T3X + A, T3X + B)

    def after_5():
        start(G0)
        passes(F3 + B, S5 + B)
        passes(B3 + A, S6 + A)

    def after_6():
        start(G1)

    def after_7():
        start(G2)
        passes(F4 + A, S7 + A)
        passes(B4 + B, S7 + B)
        got(S5 + A, S5 + B)

    def after_8():
        start(G5)
        got(S7 + A, S7 + B)

    def after_9():
        start(G7)
        got(G5)
        send_image(CF2 + B, 5)

    def after_10():
        start(G3)
        got(G7)
        send_image(CF3 + A, 7)
        send_image(CB3 + B, 7)
        got(S6 + A, S6 + B)

    def after_11():
        start(G6)

    def after_12():
        start(G4)
        got(G6)
        send_image(CB2 + A, 6)

    order = (
        (1, 0, after_1), (2, 0, after_2), (3, 0, after_3), (4, 0, after_4), (0, 1, after_5), (1, 1, after_6),
        (2, 1, after_7), (5, 2, after_8), (7, 2, after_9), (3, 1, after_10), (6, 2, after_11), (4, 1, after_12),
    )

    def step(i, carry):
        s, c = order[-1][:2]
        for k, entry in enumerate(order[:-1]):
            s = jnp.where(i == k, entry[0], s)
            c = jnp.where(i == k, entry[1], c)
        pl.when(c < 2)(lambda: half_tile(s, c))
        pl.when(c == 2)(lambda: whole_tile(s))
        for k, entry in enumerate(order):
            pl.when(i == k)(entry[2])
        return carry

    lax.fori_loop(0, len(order), step, 0)

    def loss_terms(r):
        names = [LOSS + i for i, entry in enumerate(LOSSES) if entry[0] == r]
        got(*names)
        terms = [lout[r]] + [lin[name - LOSS] for name in names]
        while len(terms) > 1:
            terms = [a + b for a, b in zip(terms[::2], terms[1::2])]
        return terms[0]

    def send_loss(r, total):
        lout[r] = total
        start(*[LOSS + i for i, entry in enumerate(LOSSES) if entry[0] == r])

    for h in (A, B):
        send_text(X1 + h, SIDE_FAR)
    for h in (A, B):
        send_text(Y1U + h, SIDE_UP)
        send_text(Y1D + h, SIDE_DOWN)
    send_loss(0, sum(lacc[:, c : c + 128] for c in range(0, 2 * CHUNK, 128)))
    send_image(CF2 + A, 5, CF3)
    send_loss(1, loss_terms(0))
    send_image(CB2 + B, 6, CB3)
    got(G1, G2, G3, G4)
    send_image(CF1 + B, 3, CF2)
    send_text(Y3U + A, FAR, X1)
    send_text(X2 + A, SIDE, Y1U, Y1D)
    send_loss(2, loss_terms(1))
    send_image(CB1 + A, 4, CB2)
    send_text(Y3D + B, FAR, X1)
    send_text(Y0U + B, UP)
    send_text(Y0D + A, DOWN)
    send_image(CF1 + A, 3, CF2)
    send_image(CB1 + B, 4, CB2)
    send_loss(3, loss_terms(2))
    send_text(X2 + B, SIDE, Y1U, Y1D)
    send_image(CF0 + B, 1, CF1)
    send_image(CB0 + A, 2, CB1)
    send_loss(4, loss_terms(3))
    send_text(Y0U + A, UP, Y3U)
    send_text(Y0D + B, DOWN, Y3D)
    send_image(CF0 + A, 1, CF1)
    send_image(CB0 + B, 2, CB1)

    def finish(i, total, ref, *more):
        for m in more:
            got(m + A, m + B)
            total += arrived[SUMS[m][0]].astype(F32)
        ref[...] = back_norm(unit[i], unit_rows(raw[i])[1], total)

    got(G0)
    finish(0, gI[0] + rI[0], gimg_ref, CF0, CB0)
    finish(1, gT[:ROWS], gtxt_ref, X2, Y0U, Y0D)
    total = loss_terms(4)
    batch = ROWS * lax.axis_size("group") * lax.axis_size("loop")
    loss_ref[...] = jnp.sum(total, keepdims=True).reshape(1, 1) / batch
    for name in SENT:
        copy(name).wait_send()


def body(images, texts, logit_scale, logit_bias):
    vmem = pl.BlockSpec(memory_space=pltpu.VMEM)
    smem = pl.BlockSpec(memory_space=pltpu.SMEM)
    hbm = pl.BlockSpec(memory_space=pl.ANY)
    block = (ROWS, WIDTH)
    loss, grad_images, grad_texts = pl.pallas_call(
        kernel,
        out_shape=(
            jax.ShapeDtypeStruct((1, 1), F32),
            jax.ShapeDtypeStruct(block, F32),
            jax.ShapeDtypeStruct(block, F32),
        ),
        in_specs=[smem, smem, hbm, hbm],
        out_specs=(vmem, vmem, vmem),
        scratch_shapes=[
            pltpu.VMEM((2,) + block, LOW),
            pltpu.VMEM((2,) + block, F32),
            pltpu.VMEM((8, 2 * ROWS, WIDTH), LOW),
            pltpu.VMEM((8 * ROWS, WIDTH), LOW),
            pltpu.VMEM((8,) + block, F32),
            pltpu.VMEM((8,) + block, F32),
            pltpu.VMEM((8,) + block, F32),
            pltpu.VMEM((8 * ROWS, WIDTH), F32),
            pltpu.VMEM((15,) + block, LOW),
            pltpu.VMEM((15,) + block, LOW),
            pltpu.VMEM((8, 2 * CHUNK), F32),
            pltpu.VMEM((len(ROUNDS), 8, 128), F32),
            pltpu.VMEM((len(LOSSES), 8, 128), F32),
            pltpu.SemaphoreType.DMA((2,)),
            pltpu.SemaphoreType.DMA((LAST,)),
            pltpu.SemaphoreType.DMA((LAST,)),
        ],
        compiler_params=pltpu.CompilerParams(
            collective_id=0, has_side_effects=True, vmem_limit_bytes=60 * 2**20
        ),
    )(logit_scale, logit_bias, images, texts)
    return loss.reshape(()), grad_images, grad_texts


def solution(mesh):
    rows = P(("group", "loop"), None)
    return jax.shard_map(
        body,
        mesh=mesh,
        in_specs=(rows, rows, P(), P()),
        out_specs=(P(), rows, rows),
        check_vma=False,
    )
```

```python
import jax
import jax.numpy as jnp
from jax import lax
from jax.experimental import pallas as pl
from jax.experimental.pallas import tpu as pltpu
from jax.sharding import PartitionSpec as P

MESH = pl.DeviceIdType.MESH
F32 = jnp.float32
LOW = jnp.bfloat16
ROWS = 128
HALF = 64
WIDTH = 1152
CHUNK = 4 * ROWS
NT = (((1,), (1,)), ((), ()))
NN = (((1,), (0,)), ((), ()))
TN = (((0,), (0,)), ((), ()))
A, B = 0, 1
(
    NEXT, PREV, BACK, UNBACK, YUP, YDOWN, YFAR, CORE, LO, MIRROR, XFAR, ZPAIR, Z2, Z4, Z6, DEVICES,
) = range(16)
(
    F1, F2, F3, F4, B1, B2, B3, B4, S0, S1, S2, S3, S4, S5, S6, S7, G0, G1, G2, G3, G4, G5, G6, G7,
    TU, TD, TX, TXU, TXD, T2, T3X, CF0, CF1, CF2, CF3, CB0, CB1, CB2, CB3,
    X1, X2, Y1U, Y1D, Y0U, Y0D, Y3U, Y3D,
    LOSS,
) = range(0, 96, 2)
LAST = LOSS + 11
HALVED = (
    F1, F2, F3, B1, B2, B3, S0, S1, S2, S3, S4, S5, S6, S7, TU, TD, TX, TXU, TXD, T2, T3X,
    CF0, CF1, CF2, CB0, CB1, CB2, X1, X2, Y1U, Y1D, Y0U, Y0D,
)
SENT = (
    [hop + h for hop in HALVED for h in (A, B)]
    + [F4 + A, B4 + B, CF3 + A, CB3 + B, Y3U + A, Y3D + B]
    + list(range(G0, G7 + 1, 2))
    + list(range(LOSS, LAST))
)
VISITS = {
    F1: (0, 1, NEXT), F2: (1, 3, NEXT), F3: (3, 5, NEXT), F4: (5, 7, NEXT),
    B1: (0, 2, BACK), B2: (2, 4, PREV), B3: (4, 6, PREV), B4: (6, 7, PREV),
}
OWN, SIDE, UP, DOWN, FAR, SIDE_UP, SIDE_DOWN, SIDE_FAR = range(8)
TEXTS = {
    TU: (OWN, DOWN, YUP), TD: (OWN, UP, YDOWN), TX: (OWN, SIDE, LO),
    T2: (OWN, FAR, YFAR),
    TXU: (SIDE, SIDE_DOWN, YUP), TXD: (SIDE, SIDE_UP, YDOWN), T3X: (FAR, SIDE_FAR, LO),
}
SUMS = {
    CF0: (0, PREV), CF1: (1, PREV), CF2: (2, PREV), CF3: (3, PREV),
    CB0: (4, UNBACK), CB1: (5, NEXT), CB2: (6, NEXT), CB3: (7, NEXT),
    X1: (8, LO), X2: (9, LO), Y1U: (10, YUP), Y1D: (11, YDOWN),
    Y0U: (12, YUP), Y0D: (13, YDOWN), Y3U: (14, YUP), Y3D: (14, YDOWN),
}
ROUNDS = (
    (CORE,),
    (LO, XFAR, MIRROR),
    (YFAR, YUP, YDOWN),
    (ZPAIR,),
    (Z4, Z2, Z6),
)
LOSSES = [(r, to) for r, partners in enumerate(ROUNDS) for to in partners]


def dot(a, b, dims):
    return lax.dot_general(a, b, dims, preferred_element_type=F32)


def unit_rows(raw):
    wide = raw.astype(F32)
    norm = jnp.sqrt(jnp.sum(wide * wide, axis=1, keepdims=True) + 1e-06)
    return wide / norm, norm


def back_norm(unit, norm, grad):
    return (grad - unit * jnp.sum(unit * grad, axis=1, keepdims=True)) / norm


def devices():
    g, l = lax.axis_index("group"), lax.axis_index("loop")
    core, y, lo = g % 2, (g // 2) % 4, g // 8
    z, hi = l % 8, l // 8

    def at(lo=lo, y=y, core=core, hi=hi, z=z):
        return ((lo * 4 + y) * 2 + core, hi * 8 + z)

    def flip(bit, when):
        return jnp.where(when, 1 - bit, bit)

    up, down = (z + 1) % 8, (z + 7) % 8
    return {
        NEXT: at(lo=flip(lo, z == 7), hi=flip(hi, z == 7), z=up),
        PREV: at(lo=flip(lo, z == 0), hi=flip(hi, z == 0), z=down),
        BACK: at(lo=flip(lo, z != 0), hi=flip(hi, z != 0), z=down),
        UNBACK: at(lo=flip(lo, z != 7), hi=flip(hi, z != 7), z=up),
        YUP: at(y=(y + 1) % 4),
        YDOWN: at(y=(y + 3) % 4),
        YFAR: at(y=(y + 2) % 4),
        CORE: at(core=1 - core),
        LO: at(lo=1 - lo),
        MIRROR: at(lo=1 - lo, hi=1 - hi),
        XFAR: at(hi=1 - hi),
        ZPAIR: at(z=z + 1 - 2 * (z % 2)),
        Z2: at(z=(z + 2) % 8),
        Z4: at(z=(z + 4) % 8),
        Z6: at(z=(z + 6) % 8),
    }


def kernel(
    scale_ref, bias_ref, img_ref, txt_ref, loss_ref, gimg_ref, gtxt_ref,
    raw, unit, V, T, gI, sI, rI, gT, out, arrived, lacc, lout, lin, lsem, ssem, rsem,
):
    dev = devices()
    scale, bias = scale_ref[0], bias_ref[0]
    loads = [pltpu.make_async_copy(ref, raw.at[i], lsem.at[i]) for i, ref in enumerate((img_ref, txt_ref))]
    for load in loads:
        load.start()

    barrier = pltpu.get_barrier_semaphore()
    for to in range(DEVICES):
        pl.semaphore_signal(barrier, inc=1, device_id=dev[to], device_id_type=MESH)

    def rows(i, h):
        return pl.ds(i * ROWS + h * HALF, HALF)

    def copy(name):
        h, base = name % 2, name - name % 2
        if name >= LOSS:
            r, to = LOSSES[name - LOSS]
            src, dst = lout.at[r], lin.at[name - LOSS]
        elif base in VISITS:
            s, d, to = VISITS[base]
            src, dst = V.at[s, rows(0, h)], V.at[d, rows(0, h)]
        elif base in TEXTS:
            s, d, to = TEXTS[base]
            src, dst = T.at[rows(s, h)], T.at[rows(d, h)]
        elif base in SUMS:
            k, to = SUMS[base]
            src, dst = out.at[k, rows(0, h)], arrived.at[k, rows(0, h)]
        elif base >= G0:
            s, to = (base - G0) // 2, CORE
            src, dst = sI.at[s], rI.at[s]
        else:
            s, to = (base - S0) // 2, CORE
            src, dst = V.at[s, rows(0, h)], V.at[s, rows(1, h)]
        return pltpu.make_async_remote_copy(
            src_ref=src, dst_ref=dst, send_sem=ssem.at[name], recv_sem=rsem.at[name],
            device_id=dev[to], device_id_type=MESH,
        )

    def start(*names):
        for name in names:
            copy(name).start()

    def got(*names):
        for name in names:
            copy(name).wait_recv()

    def passes(name, *onward):
        got(name)
        start(*onward)

    def pair_terms(logits):
        w = jnp.exp(jnp.minimum(logits, 80.0))
        u = 1.0 + w
        prob = w * (1.0 / u)
        log_term = jnp.where(w < 0.01, w * (1.0 - w * (0.5 - w * (1.0 / 3.0))), jnp.log(u))
        return prob, jnp.maximum(logits, log_term)

    def tile(s, texts, own=False):
        v, t = V[s], T[texts]
        logits = scale * dot(v, t, NT) + bias
        if own:
            row = lax.broadcasted_iota(jnp.int32, logits.shape, 0)
            col = lax.broadcasted_iota(jnp.int32, logits.shape, 1)
            positive = (row == col) & (row < ROWS)
            prob, loss = pair_terms(jnp.where(positive, -logits, logits))
            prob = jnp.where(positive, -prob, prob)
        else:
            prob, loss = pair_terms(logits)
        g = (prob * scale).astype(LOW)
        lacc[:, : t.shape[0]] += jnp.sum(loss.reshape(-1, 8, t.shape[0]), axis=0)
        gT[texts] += dot(g, v, TN)
        return dot(g, t, NN)

    def half_tile(s, c, own=False):
        part = tile(s, pl.ds(pl.multiple_of(c * CHUNK, CHUNK), CHUNK), own)
        gI[s] += part[:ROWS]
        sI[s] += part[ROWS:]

    def whole_tile(s):
        part = tile(s, pl.ds(0, 2 * CHUNK))
        gI[s] = part[:ROWS]
        sI[s] = part[ROWS:]

    def send_image(name, s, *more):
        k, h = SUMS[name - name % 2][0], name % 2
        total = gI[s, rows(0, h)] + rI[s, rows(0, h)]
        for m in more:
            got(m + h)
            total += arrived[SUMS[m][0], rows(0, h)].astype(F32)
        out[k, rows(0, h)] = total.astype(LOW)
        start(name)

    def send_text(name, block, *more):
        k, h = SUMS[name - name % 2][0], name % 2
        total = gT[rows(block, h)]
        for m in more:
            got(m + h)
            total += arrived[SUMS[m][0], rows(0, h)].astype(F32)
        out[k, rows(0, h)] = total.astype(LOW)
        start(name)

    for i in range(2):
        loads[i].wait()
        unit[i] = unit_rows(raw[i])[0]
    V[0, :ROWS] = unit[0].astype(LOW)
    T[:ROWS] = unit[1].astype(LOW)
    pl.semaphore_wait(barrier, DEVICES)
    start(F1 + A, B1 + B, TU + A, TD + B, TX + A, S0 + A)
    start(F1 + B, B1 + A, TU + B, TD + A, TX + B, S0 + B)
    start(T2 + A, T2 + B)
    gT[...] = jnp.zeros_like(gT)
    gI[:5] = jnp.zeros_like(gI[:5])
    sI[:5] = jnp.zeros_like(sI[:5])
    lacc[...] = jnp.zeros_like(lacc)

    passes(F1 + A, F2 + A, S1 + A)
    passes(B1 + B, B2 + B, S2 + B)
    got(TU + A, TD + B, TU + B, TD + A, S0 + A, S0 + B)
    passes(TX + A, TXU + A, TXD + A)
    passes(TX + B, TXU + B, TXD + B)
    half_tile(0, 0, True)
    passes(F1 + B, F2 + B, S1 + B)
    passes(B1 + A, B2 + A, S2 + A)
    got(S1 + A, S1 + B)

    def after_1():
        passes(T2 + A, T3X + A)
        passes(T2 + B, T3X + B)
        passes(F2 + A, F3 + A, S3 + A)
        passes(B2 + B, B3 + B, S4 + B)
        got(S2 + A, S2 + B)

    def after_2():
        passes(F2 + B, F3 + B, S3 + B)
        passes(B2 + A, B3 + A, S4 + A)
        got(S3 + A, S3 + B)

    def after_3():
        passes(F3 + A, F4 + A, S5 + A)
        passes(B3 + B, B4 + B, S6 + B)
        got(S4 + A, S4 + B)

    def after_4():
        got(TXU + A, TXD + A, TXU + B, TXD + B, T3X + A, T3X + B)

    def after_5():
        start(G0)
        passes(F3 + B, S5 + B)
        passes(B3 + A, S6 + A)

    def after_6():
        start(G1)

    def after_7():
        start(G2)
        passes(F4 + A, S7 + A)
        passes(B4 + B, S7 + B)
        got(S5 + A, S5 + B)

    def after_8():
        start(G5)
        got(S7 + A, S7 + B)

    def after_9():
        start(G7)
        got(G5)
        send_image(CF2 + B, 5)

    def after_10():
        start(G3)
        got(G7)
        send_image(CF3 + A, 7)
        send_image(CB3 + B, 7)
        got(S6 + A, S6 + B)

    def after_11():
        start(G6)

    def after_12():
        start(G4)
        got(G6)
        send_image(CB2 + A, 6)

    order = (
        (1, 0, after_1), (2, 0, after_2), (3, 0, after_3), (4, 0, after_4), (0, 1, after_5), (1, 1, after_6),
        (2, 1, after_7), (5, 2, after_8), (7, 2, after_9), (3, 1, after_10), (6, 2, after_11), (4, 1, after_12),
    )

    def step(i, carry):
        s, c = order[-1][:2]
        for k, entry in enumerate(order[:-1]):
            s = jnp.where(i == k, entry[0], s)
            c = jnp.where(i == k, entry[1], c)
        pl.when(c < 2)(lambda: half_tile(s, c))
        pl.when(c == 2)(lambda: whole_tile(s))
        for k, entry in enumerate(order):
            pl.when(i == k)(entry[2])
        return carry

    lax.fori_loop(0, len(order), step, 0)

    def loss_terms(r):
        names = [LOSS + i for i, entry in enumerate(LOSSES) if entry[0] == r]
        got(*names)
        terms = [lout[r]] + [lin[name - LOSS] for name in names]
        while len(terms) > 1:
            terms = [a + b for a, b in zip(terms[::2], terms[1::2])]
        return terms[0]

    def send_loss(r, total):
        lout[r] = total
        start(*[LOSS + i for i, entry in enumerate(LOSSES) if entry[0] == r])

    for h in (A, B):
        send_text(X1 + h, SIDE_FAR)
    for h in (A, B):
        send_text(Y1U + h, SIDE_UP)
        send_text(Y1D + h, SIDE_DOWN)
    send_loss(0, sum(lacc[:, c : c + 128] for c in range(0, 2 * CHUNK, 128)))
    send_image(CF2 + A, 5, CF3)
    send_loss(1, loss_terms(0))
    send_image(CB2 + B, 6, CB3)
    got(G1, G2, G3, G4)
    send_image(CF1 + B, 3, CF2)
    send_text(Y3U + A, FAR, X1)
    send_text(X2 + A, SIDE, Y1U, Y1D)
    send_loss(2, loss_terms(1))
    send_image(CB1 + A, 4, CB2)
    send_text(Y3D + B, FAR, X1)
    send_text(Y0U + B, UP)
    send_text(Y0D + A, DOWN)
    send_image(CF1 + A, 3, CF2)
    send_image(CB1 + B, 4, CB2)
    send_loss(3, loss_terms(2))
    send_text(X2 + B, SIDE, Y1U, Y1D)
    send_image(CF0 + B, 1, CF1)
    send_image(CB0 + A, 2, CB1)
    send_loss(4, loss_terms(3))
    send_text(Y0U + A, UP, Y3U)
    send_text(Y0D + B, DOWN, Y3D)
    send_image(CF0 + A, 1, CF1)
    send_image(CB0 + B, 2, CB1)

    def finish(i, total, ref, *more):
        for m in more:
            got(m + A, m + B)
            total += arrived[SUMS[m][0]].astype(F32)
        ref[...] = back_norm(unit[i], unit_rows(raw[i])[1], total)

    finish(1, gT[:ROWS], gtxt_ref, X2, Y0U, Y0D)
    total = loss_terms(4)
    batch = ROWS * lax.axis_size("group") * lax.axis_size("loop")
    loss_ref[...] = jnp.sum(total, keepdims=True).reshape(1, 1) / batch
    for name in SENT:
        copy(name).wait_send()
    got(G0)
    finish(0, gI[0] + rI[0], gimg_ref, CF0, CB0)


def body(images, texts, logit_scale, logit_bias):
    vmem = pl.BlockSpec(memory_space=pltpu.VMEM)
    smem = pl.BlockSpec(memory_space=pltpu.SMEM)
    hbm = pl.BlockSpec(memory_space=pl.ANY)
    block = (ROWS, WIDTH)
    loss, grad_images, grad_texts = pl.pallas_call(
        kernel,
        out_shape=(
            jax.ShapeDtypeStruct((1, 1), F32),
            jax.ShapeDtypeStruct(block, F32),
            jax.ShapeDtypeStruct(block, F32),
        ),
        in_specs=[smem, smem, hbm, hbm],
        out_specs=(vmem, vmem, vmem),
        scratch_shapes=[
            pltpu.VMEM((2,) + block, LOW),
            pltpu.VMEM((2,) + block, F32),
            pltpu.VMEM((8, 2 * ROWS, WIDTH), LOW),
            pltpu.VMEM((8 * ROWS, WIDTH), LOW),
            pltpu.VMEM((8,) + block, F32),
            pltpu.VMEM((8,) + block, F32),
            pltpu.VMEM((8,) + block, F32),
            pltpu.VMEM((8 * ROWS, WIDTH), F32),
            pltpu.VMEM((15,) + block, LOW),
            pltpu.VMEM((15,) + block, LOW),
            pltpu.VMEM((8, 2 * CHUNK), F32),
            pltpu.VMEM((len(ROUNDS), 8, 128), F32),
            pltpu.VMEM((len(LOSSES), 8, 128), F32),
            pltpu.SemaphoreType.DMA((2,)),
            pltpu.SemaphoreType.DMA((LAST,)),
            pltpu.SemaphoreType.DMA((LAST,)),
        ],
        compiler_params=pltpu.CompilerParams(
            collective_id=0, has_side_effects=True, vmem_limit_bytes=60 * 2**20
        ),
    )(logit_scale, logit_bias, images, texts)
    return loss.reshape(()), grad_images, grad_texts


def solution(mesh):
    rows = P(("group", "loop"), None)
    return jax.shard_map(
        body,
        mesh=mesh,
        in_specs=(rows, rows, P(), P()),
        out_specs=(P(), rows, rows),
        check_vma=False,
    )
```
